32 devices in a mesh: parts: 2 (over x), pool: 16 (over z, y, core).
Axes of the slice: x: 2, y: 2, z: 4, core: 2. Of those that a mesh axis runs over, the one named last changes fastest.
Arguments:
- queries: bfloat16 [64, 16384], P('parts', 'pool'), parts along dimension 0, as said below
- kv_pages: bfloat16 [512, 128, 2048], P(('parts', 'pool')), parts along dimension 0, may hold values from -6 to 6
- page_table: int32 [64, 8], P('parts'), parts along dimension 0, may hold values from -1 to 255, as said below
- lengths: int32 [64], P('parts'), parts along dimension 0, may hold values from 1 to 1024, as said below
- out_weight: bfloat16 [16384, 16384], P('pool'), may hold values from -0.5 to 0.5
Outputs:
- projected: bfloat16 [64, 16384], P('parts', 'pool'), parts along dimension 0
The draws below stay inside these ranges and needn't reach their ends.
There are 2 independent parts, one for each index of `parts`. The reference program is written for one: setup_inputs(seed, part) draws one part's arguments, and reference() takes and returns one part's arrays. A program takes and returns all parts, laid end to end along the dimension named above; an argument that names none is the same for every part. Nothing has to cross between parts.
Inputs may be any that keep to these rules, and one draw needn't show every extreme that they name: `page_table`: row s holds ceil(lengths[s] / 128) distinct slot numbers followed by -1; no slot is named twice in the table; slot g lies on pool device g // 16. `lengths`: some sequence has exactly 1024 tokens. `queries`: real values; entries of some heads may be large.
All inputs are finite; a program needn't handle non-finite values.
Results may differ from the reference program's by a relative error of at most 0.009.
Values may be sent and summed in bfloat16 or wider, within the bound.
A program may use at most 128 MiB of HBM per device.

```python
import jax
import jax.numpy as jnp
from jax import lax

D = 16384
HEADS = 128
KV_HEADS = 8
HEAD_DIM = 128
PAGE = 128
SEQS = 32
PAGES = 256
MAXP = 8


def layout_tables(key):
    base = jax.random.fold_in(key, 11)
    first, second, third, fourth = jax.random.split(base, 4)
    lowest = max(1, 3 * MAXP // 4)
    counts = jax.random.randint(first, (SEQS,), lowest, MAXP + 1)
    longest = jax.random.randint(second, (), 0, SEQS)
    places = jnp.arange(SEQS, dtype=jnp.int32)
    counts = jnp.where(places == longest, MAXP, counts).astype(jnp.int32)
    shorter = (longest + 1) % SEQS
    counts = jnp.where(places == shorter, jnp.minimum(counts, MAXP - 1), counts).astype(jnp.int32)
    trims = jax.random.randint(third, (SEQS,), 0, PAGE)
    trims = jnp.where(places == longest, 0, trims).astype(jnp.int32)
    order = jax.random.permutation(fourth, PAGES).astype(jnp.int32)
    order = ((order - order[0] + PAGES - 1) % PAGES).astype(jnp.int32)
    starts = jnp.cumsum(counts) - counts
    columns = jnp.arange(MAXP, dtype=jnp.int32)
    where_at = jnp.clip(starts[:, None] + columns[None, :], 0, PAGES - 1)
    table = jnp.where(columns[None, :] < counts[:, None], order[where_at], -1).astype(jnp.int32)
    lengths = (counts * PAGE - trims).astype(jnp.int32)
    return (table, lengths)


def draw_page_table(key, part):
    return layout_tables(key)[0]


def draw_lengths(key, part):
    return layout_tables(key)[1]


def draw_queries(key, part):
    key = jax.random.fold_in(key, 5)
    first = jax.random.fold_in(key, 0)
    values = jnp.clip(jax.random.normal(first, (SEQS, HEADS, HEAD_DIM), jnp.float32), -6.0, 6.0)
    return values.reshape(SEQS, HEADS * HEAD_DIM).astype(jnp.bfloat16)


def levels(stream_key, shape, cuts, low, high):
    def one(axis_at, blocks):
        heights = jax.random.uniform(jax.random.fold_in(jax.random.fold_in(stream_key, 6), axis_at), (blocks,), jnp.float32, low / len(cuts), high / len(cuts))
        return jnp.repeat(jnp.exp(heights), shape[axis_at] // blocks).reshape((-1,) + (1,) * (len(shape) - axis_at - 1))

    level = one(*cuts[0])
    for cut in cuts[1:]:
        level = level * one(*cut)
    return level


def normal_values(stream_key, extent, scale, limit, cuts=(), kind=jnp.bfloat16):
    drawn = scale * jax.random.normal(stream_key, extent, jnp.float32)
    if cuts:
        drawn = drawn * levels(stream_key, extent, cuts, -0.22, 0.18)
    return jnp.clip(drawn, -limit, limit).astype(kind)


def setup_inputs(seed: int = 0, part: int = 0) -> dict:
    streams_of = jax.random.split(jax.random.key(seed), 6)
    part_keys = jax.random.split(jax.random.fold_in(streams_of[5], part), 6)
    queries = draw_queries(jax.random.fold_in(jax.random.fold_in(streams_of[5], part), 71), part)
    kv_pages = normal_values(part_keys[1], (PAGES, PAGE, 2 * KV_HEADS * HEAD_DIM), 1.0, 6.0, ((0, 16),))
    page_table = draw_page_table(jax.random.fold_in(jax.random.fold_in(streams_of[5], part), 71), part)
    lengths = draw_lengths(jax.random.fold_in(jax.random.fold_in(streams_of[5], part), 71), part)
    out_weight = normal_values(streams_of[4], (HEADS * HEAD_DIM, D), HEADS ** -0.5, 0.5, ((0, 16),))
    return {"queries": queries, "kv_pages": kv_pages, "page_table": page_table, "lengths": lengths, "out_weight": out_weight}


NEG_FILL = -1.0e30


def attend_one(packed, kv_pages):
    query, table_row, length = packed
    width = KV_HEADS * HEAD_DIM
    group = HEADS // KV_HEADS
    slot_rows = jnp.maximum(table_row, 0).astype(jnp.int32)
    chosen = kv_pages[slot_rows].reshape(MAXP * PAGE, 2 * width)
    key_rows = chosen[:, :width].reshape(MAXP * PAGE, KV_HEADS, HEAD_DIM).astype(jnp.float32)
    value_rows = chosen[:, width:].reshape(MAXP * PAGE, KV_HEADS, HEAD_DIM).astype(jnp.float32)
    query_rows = query.reshape(KV_HEADS, group, HEAD_DIM).astype(jnp.float32)
    scores = jnp.einsum('kgd,tkd->kgt', query_rows, key_rows) * (HEAD_DIM ** -0.5)
    visible = jnp.arange(MAXP * PAGE, dtype=jnp.int32) < length
    scores = jnp.where(visible[None, None, :], scores, NEG_FILL)
    top = jnp.max(scores, axis=2)
    weights = jnp.exp(scores - top[:, :, None])
    total = jnp.sum(weights, axis=2)
    rounded = lax.optimization_barrier(weights.astype(jnp.bfloat16)).astype(jnp.float32)
    accum = jnp.einsum('kgt,tkd->kgd', rounded, value_rows)
    return (accum / total[:, :, None]).astype(jnp.bfloat16).reshape(HEADS * HEAD_DIM)


def reference(queries, kv_pages, page_table, lengths, out_weight):
    attended = lax.map(lambda packed: attend_one(packed, kv_pages), (queries, page_table, lengths))
    return jnp.dot(attended, out_weight, preferred_element_type=jnp.float32).astype(jnp.bfloat16)
```

```python
import functools

import jax
import jax.numpy as jnp
from jax import lax
from jax.experimental import pallas as pl
from jax.experimental.pallas import tpu as pltpu
from jax.sharding import PartitionSpec as P

HEADS = 128
KV_HEADS = 8
HEAD_DIM = 128
GROUP = HEADS // KV_HEADS
NEG = -1e30
F32 = jnp.float32
BF16 = jnp.bfloat16


def grid_of(n):
    chips = n // 2
    outer = 1
    while outer * outer < chips:
        outer *= 2
    return outer, chips // outer


def kernel(
    n, q_ref, kv_hbm, pages_ref, tiled_ref, left_ref, w_hbm, out_ref,
    kv, w, qall, pick, mask, perm, att,
    acc_send, acc_recv, ml_send, ml_recv,
    part1_send, part1_recv, part2_send, part2_recv, part3_send, part3_recv, total,
    kv_sem, w_sem, q_ssem, q_rsem, acc_ssem, acc_rsem, ml_ssem, ml_rsem,
    s1_ssem, s1_rsem, s2_ssem, s2_rsem, s3_ssem, s3_rsem,
):
    A, B = grid_of(n)
    me = lax.axis_index("pool")
    c = lax.rem(me, 2)
    b = lax.rem(me // 2, B)
    a = me // (2 * B)
    slots, page_len = kv.shape[0], kv.shape[1]
    seqs = q_ref.shape[0]
    max_pages = pages_ref.shape[1]
    own_heads = HEADS // n
    padded = max(own_heads, 8)
    owners = n // KV_HEADS
    rows = own_heads * seqs
    cols = w.shape[1] // n

    def index(x, y, z):
        return (lax.rem(x, A) * B + lax.rem(y, B)) * 2 + z

    def remote(src, dst, ssem, rsem, to):
        return pltpu.make_async_remote_copy(
            src_ref=src, dst_ref=dst, send_sem=ssem, recv_sem=rsem,
            device_id={"pool": to}, device_id_type=pl.DeviceIdType.MESH,
        )

    def kv_copy(p):
        return pltpu.make_async_copy(kv_hbm.at[p], kv.at[p], kv_sem.at[p])

    def w_copy(d):
        span = pl.ds(pl.multiple_of(d * cols, 128), cols)
        return pltpu.make_async_copy(w_hbm.at[:, span], w.at[:, span], w_sem.at[d])

    barrier = pltpu.get_barrier_semaphore()
    for step in range(1, n):
        pl.semaphore_signal(
            barrier, inc=1, device_id={"pool": lax.rem(me + step, n)},
            device_id_type=pl.DeviceIdType.MESH,
        )
    for p in range(slots):
        kv_copy(p).start()

    def q_block(i):
        return qall.at[pl.ds(pl.multiple_of(i * rows, 32), rows), :]

    for h in range(own_heads):
        qall[pl.ds(pl.multiple_of(me * rows + h * seqs, 32), seqs), :] = q_ref[
            :, h * HEAD_DIM : (h + 1) * HEAD_DIM
        ]
    pl.semaphore_wait(barrier, n - 1)

    mate = index(a, b, 1 - c)
    sent = []

    def q_send(i, to):
        copy = remote(q_block(i), q_block(i), q_ssem.at[len(sent)], q_rsem.at[i], to)
        copy.start()
        sent.append(copy)

    def q_wait(i):
        remote(q_block(i), q_block(i), q_ssem.at[0], q_rsem.at[i], mate).wait_recv()

    for ra in range(1, A):
        q_send(me, index(a + ra, b, c))
    for rb in range(1, B):
        q_send(me, index(a, b + rb, c))
    q_send(me, mate)
    for d in range(n):
        w_copy(d).start()

    lane = lax.broadcasted_iota(jnp.int32, (max_pages, page_len), 1)
    rowh = lax.broadcasted_iota(jnp.int32, (GROUP, GROUP * seqs), 0)
    laneh = lax.broadcasted_iota(jnp.int32, (GROUP, GROUP * seqs), 1) // seqs
    token = lax.broadcasted_iota(jnp.int32, (GROUP, page_len), 1).astype(F32)

    def build(p, carry):
        hit = tiled_ref[...] == me * slots + p
        owned = jnp.max(jnp.where(hit, 1.0, 0.0), axis=0, keepdims=True)
        place = pl.ds(pl.multiple_of(p * GROUP, GROUP), GROUP)
        pick[place, :] = jnp.where(rowh == laneh, owned, 0.0).astype(BF16)
        left = jnp.where(
            jnp.logical_and(hit[:, :page_len], lane < seqs), left_ref[:, :page_len], 0
        ).astype(F32)
        left = jnp.sum(jnp.sum(left, axis=0, keepdims=True), axis=1, keepdims=True)
        mask[place, :] = jnp.where(token < left, 1.0, 0.0)
        return carry

    lax.fori_loop(0, slots, build, 0)
    count = slots * GROUP
    to_row = lax.broadcasted_iota(jnp.int32, (count, count), 0)
    from_row = lax.broadcasted_iota(jnp.int32, (count, count), 1)
    perm[...] = jnp.where(
        jnp.logical_and(to_row // slots == from_row % GROUP, to_row % slots == from_row // GROUP),
        1.0, 0.0,
    ).astype(BF16)

    for ra in range(1, A):
        i = index(a + ra, b, c)
        q_wait(i)
        for rb in range(1, B):
            q_send(i, index(a, b + rb, c))
        q_send(i, mate)
    for ra in range(A):
        for rb in range(1, B):
            i = index(a + ra, b + rb, c)
            q_wait(i)
            q_send(i, mate)
    for ra in range(A):
        for rb in range(B):
            q_wait(index(a + ra, b + rb, 1 - c))
    for p in range(slots):
        kv_copy(p).wait()

    spread = jnp.where(
        lax.broadcasted_iota(jnp.int32, (slots, 1, 128), 2)
        == lax.rem(me * slots, 128) + lax.broadcasted_iota(jnp.int32, (slots, 1, 128), 0),
        1.0, 0.0,
    )
    block = own_heads * slots

    def acc_copy(o):
        return remote(
            acc_send.at[pl.ds(pl.multiple_of(o * block, 16), block), :], acc_recv.at[me],
            acc_ssem.at[o], acc_rsem.at[me], o,
        )

    def ml_copy(o):
        return remote(ml_send.at[o], ml_recv.at[me], ml_ssem.at[o], ml_rsem.at[me], o)

    ml_send[...] = jnp.zeros_like(ml_send)
    first = me // owners

    def attend(t, carry):
        k = lax.rem(first + t, KV_HEADS)
        at = pl.multiple_of(k * HEAD_DIM, HEAD_DIM)
        mine = qall[pl.ds(pl.multiple_of(k * GROUP * seqs, GROUP * seqs), GROUP * seqs), :]
        query = jnp.dot(pick[...], mine, preferred_element_type=F32).astype(BF16)
        query = query.reshape(slots, GROUP, HEAD_DIM)
        keys = kv[:, :, pl.ds(at, HEAD_DIM)]
        values = kv[:, :, pl.ds(pl.multiple_of(KV_HEADS * HEAD_DIM + at, 128), HEAD_DIM)]
        score = jnp.einsum("phd,ptd->pht", query, keys, preferred_element_type=F32)
        seen = mask[...].reshape(slots, GROUP, page_len)
        score = jnp.where(seen > 0, score * HEAD_DIM**-0.5, NEG)
        top = jnp.max(score, axis=2, keepdims=True)
        weight = jnp.exp(score - top) * seen
        share = jnp.sum(weight, axis=2, keepdims=True)
        acc = jnp.einsum("pht,ptd->phd", weight.astype(BF16), values, preferred_element_type=F32)
        acc = jnp.dot(
            perm[...], acc.reshape(count, HEAD_DIM).astype(BF16), preferred_element_type=F32
        )
        acc_send[pl.ds(pl.multiple_of(k * count, count), count), :] = acc.astype(BF16)
        top = jnp.sum(top * spread, axis=0)
        share = jnp.sum(share * spread, axis=0)
        for j in range(owners):
            o = k * owners + j
            ml_send[o, 0:own_heads, :] = top[j * own_heads : (j + 1) * own_heads]
            ml_send[o, padded : padded + own_heads, :] = share[j * own_heads : (j + 1) * own_heads]

            @pl.when(o != me)
            def _():
                acc_copy(o).start()
                ml_copy(o).start()

        return carry

    lax.fori_loop(0, KV_HEADS, attend, 0)
    acc_recv[me] = acc_send[pl.ds(pl.multiple_of(me * block, 16), block), :]
    ml_recv[me] = ml_send[me]

    for step in range(1, n):
        i = lax.rem(me + step, n)
        remote(acc_recv.at[i], acc_recv.at[i], acc_ssem.at[i], acc_rsem.at[i], i).wait_recv()
        remote(ml_recv.at[i], ml_recv.at[i], ml_ssem.at[i], ml_rsem.at[i], i).wait_recv()

    all_slots = n * slots
    slot_id = lax.broadcasted_iota(jnp.int32, (seqs, all_slots), 1)
    named = jnp.zeros((seqs, all_slots), F32)
    for j in range(max_pages):
        named = jnp.where(pages_ref[:, j : j + 1] == slot_id, 1.0, named)
    per = 128 // slots
    ml_all = jnp.concatenate(
        [jnp.sum(ml_recv[g * per : (g + 1) * per], axis=0) for g in range(n // per)], axis=1
    )
    for h in range(own_heads):
        top_row = ml_all[h : h + 1, :]
        share_row = ml_all[padded + h : padded + h + 1, :]
        top = jnp.max(jnp.where(named > 0, top_row, -3e38), axis=1, keepdims=True)
        scale = jnp.where(named > 0, jnp.exp(jnp.minimum(top_row - top, 0.0)), 0.0).astype(BF16)
        whole = jnp.sum(scale.astype(F32) * share_row, axis=1, keepdims=True)
        acc = acc_recv[:, h * slots : (h + 1) * slots, :].reshape(all_slots, HEAD_DIM)
        acc = jnp.dot(scale, acc, preferred_element_type=F32)
        att[:, h * HEAD_DIM : (h + 1) * HEAD_DIM] = (acc / whole).astype(BF16)

    tile = min(cols, 256)

    def project(d, put):
        w_copy(d).wait()

        def one(j, carry):
            at = pl.ds(pl.multiple_of(d * cols + j * tile, 128), tile)
            put(
                pl.ds(pl.multiple_of(j * tile, 128), tile),
                jnp.dot(att[...], w[:, at], preferred_element_type=F32),
            )
            return carry

        lax.fori_loop(0, cols // tile, one, 0)

    def part1(t):
        return remote(part1_send.at[t], part1_recv.at[t], s1_ssem.at[t], s1_rsem.at[t], mate)

    def part2(ra, rb):
        t = ra * (B - 1) + rb - 1
        return remote(
            part2_send.at[t], part2_recv.at[t], s2_ssem.at[t], s2_rsem.at[t],
            index(a, b + rb, c),
        )

    def part3(ra):
        t = ra - 1
        return remote(
            part3_send.at[t], part3_recv.at[t], s3_ssem.at[t], s3_rsem.at[t],
            index(a + ra, b, c),
        )

    order = [(ra, rb) for rb in list(range(1, B)) + [0] for ra in list(range(1, A)) + [0]]
    for ra, rb in order:
        t = ra * B + rb

        def put(at, value):
            part1_send[t, :, at] = value.astype(BF16)

        project(index(a + ra, b + rb, 1 - c), put)
        part1(t).start()
    for ra, rb in order:
        t = ra * B + rb

        def put(at, value):
            total[:, at] = value

        project(index(a + ra, b + rb, c), put)
        part1(t).wait_recv()
        value = total[...] + part1_recv[t].astype(F32)
        if rb:
            part2_send[ra * (B - 1) + rb - 1] = value.astype(BF16)
            part2(ra, rb).start()
            continue
        for other in range(1, B):
            part2(ra, other).wait_recv()
            value = value + part2_recv[ra * (B - 1) + other - 1].astype(F32)
        if ra:
            part3_send[ra - 1] = value.astype(BF16)
            part3(ra).start()
            continue
        for other in range(1, A):
            part3(other).wait_recv()
            value = value + part3_recv[other - 1].astype(F32)
        out_ref[...] = value.astype(BF16)

    for copy in sent:
        copy.wait_send()
    for step in range(1, n):
        o = lax.rem(me + step, n)
        acc_copy(o).wait_send()
        ml_copy(o).wait_send()
    for ra, rb in order:
        part1(ra * B + rb).wait_send()
        if rb:
            part2(ra, rb).wait_send()
        elif ra:
            part3(ra).wait_send()


def shards(n, queries, kv_pages, page_table, lengths, out_weight):
    slots, page_len, width = kv_pages.shape
    seqs, max_pages = page_table.shape
    A, B = grid_of(n)
    own_heads = HEADS // n
    padded = max(own_heads, 8)
    depth, features = out_weight.shape
    cols = features // n
    block = own_heads * slots
    tiled = jnp.tile(page_table.T, (1, GROUP))
    left = lengths[None, :] - page_len * jnp.arange(max_pages, dtype=jnp.int32)[:, None]
    left = jnp.tile(left, (1, GROUP))
    vmem = pl.BlockSpec(memory_space=pltpu.VMEM)
    hbm = pl.BlockSpec(memory_space=pl.ANY)
    dma = pltpu.SemaphoreType.DMA
    q_sends = (A - 1) + (B - 1) + 1 + (A - 1) * B + A * (B - 1)
    return pl.pallas_call(
        functools.partial(kernel, n),
        out_shape=jax.ShapeDtypeStruct((seqs, cols), BF16),
        in_specs=[vmem, hbm, vmem, vmem, vmem, hbm],
        out_specs=vmem,
        scratch_shapes=[
            pltpu.VMEM((slots, page_len, width), BF16),
            pltpu.VMEM((depth, features), BF16),
            pltpu.VMEM((HEADS * seqs, HEAD_DIM), BF16),
            pltpu.VMEM((slots * GROUP, GROUP * seqs), BF16),
            pltpu.VMEM((slots * GROUP, page_len), F32),
            pltpu.VMEM((slots * GROUP, slots * GROUP), BF16),
            pltpu.VMEM((seqs, depth), BF16),
            pltpu.VMEM((HEADS * slots, HEAD_DIM), BF16),
            pltpu.VMEM((n, block, HEAD_DIM), BF16),
            pltpu.VMEM((n, 2 * padded, 128), F32),
            pltpu.VMEM((n, 2 * padded, 128), F32),
            pltpu.VMEM((A * B, seqs, cols), BF16),
            pltpu.VMEM((A * B, seqs, cols), BF16),
            pltpu.VMEM((A * (B - 1), seqs, cols), BF16),
            pltpu.VMEM((A * (B - 1), seqs, cols), BF16),
            pltpu.VMEM((A - 1, seqs, cols), BF16),
            pltpu.VMEM((A - 1, seqs, cols), BF16),
            pltpu.VMEM((seqs, cols), F32),
            dma((slots,)), dma((n,)), dma((q_sends,)), dma((n,)),
            dma((n,)), dma((n,)), dma((n,)), dma((n,)),
            dma((A * B,)), dma((A * B,)),
            dma((A * (B - 1),)), dma((A * (B - 1),)),
            dma((A - 1,)), dma((A - 1,)),
        ],
        compiler_params=pltpu.CompilerParams(
            collective_id=0, has_side_effects=True, vmem_limit_bytes=60 * 1024 * 1024
        ),
        name="paged_decode",
    )(queries, kv_pages, page_table, tiled, left, out_weight)


def solution(mesh):
    placed = (
        P("parts", "pool"),
        P(("parts", "pool"), None, None),
        P("parts", None),
        P("parts"),
        P("pool", None),
    )
    return jax.shard_map(
        functools.partial(shards, mesh.shape["pool"]), mesh=mesh, in_specs=placed,
        out_specs=P("parts", "pool"), check_vma=False,
    )
```

```python
import functools

import jax
import jax.numpy as jnp
from jax import lax
from jax.experimental import pallas as pl
from jax.experimental.pallas import tpu as pltpu
from jax.sharding import PartitionSpec as P

HEADS = 128
KV_HEADS = 8
HEAD_DIM = 128
GROUP = HEADS // KV_HEADS
NEG = -1e30
F32 = jnp.float32
BF16 = jnp.bfloat16


def grid_of(n):
    chips = n // 2
    outer = 1
    while outer * outer < chips:
        outer *= 2
    return outer, chips // outer


def kernel(
    n, q_ref, kv_hbm, pages_ref, w_hbm, out_ref,
    kv, w, qall, pick, mask, perm, att,
    acc_send, acc_recv, ml_send, ml_recv,
    part1_send, part1_recv, part2_send, part2_recv, part3_send, part3_recv,
    kv_sem, w_sem, q_ssem, q_rsem, acc_ssem, acc_rsem, ml_ssem, ml_rsem,
    s1_ssem, s1_rsem, s2_ssem, s2_rsem, s3_ssem, s3_rsem,
):
    A, B = grid_of(n)
    me = lax.axis_index("pool")
    c = lax.rem(me, 2)
    b = lax.rem(me // 2, B)
    a = me // (2 * B)
    slots, page_len = kv.shape[0], kv.shape[1]
    seqs = q_ref.shape[0]
    max_pages = pages_ref.shape[1] - 1
    own_heads = HEADS // n
    padded = max(own_heads, 8)
    owners = n // KV_HEADS
    rows = own_heads * seqs
    cols = w.shape[1] // n

    def index(x, y, z):
        return (lax.rem(x, A) * B + lax.rem(y, B)) * 2 + z

    def remote(src, dst, ssem, rsem, to):
        return pltpu.make_async_remote_copy(
            src_ref=src, dst_ref=dst, send_sem=ssem, recv_sem=rsem,
            device_id={"pool": to}, device_id_type=pl.DeviceIdType.MESH,
        )

    def kv_copy(p):
        return pltpu.make_async_copy(kv_hbm.at[p], kv.at[p], kv_sem.at[p])

    def w_copy(d):
        span = pl.ds(pl.multiple_of(d * cols, 128), cols)
        return pltpu.make_async_copy(w_hbm.at[:, span], w.at[:, span], w_sem.at[d])

    barrier = pltpu.get_barrier_semaphore()
    for step in range(1, n):
        pl.semaphore_signal(
            barrier, inc=1, device_id={"pool": lax.rem(me + step, n)},
            device_id_type=pl.DeviceIdType.MESH,
        )
    for p in range(slots):
        kv_copy(p).start()

    def q_block(i):
        return qall.at[pl.ds(pl.multiple_of(i * rows, 32), rows), :]

    for h in range(own_heads):
        qall[pl.ds(pl.multiple_of(me * rows + h * seqs, 32), seqs), :] = q_ref[
            :, h * HEAD_DIM : (h + 1) * HEAD_DIM
        ]
    pl.semaphore_wait(barrier, n - 1)

    mate = index(a, b, 1 - c)
    sent = []

    def q_send(i, to):
        copy = remote(q_block(i), q_block(i), q_ssem.at[len(sent)], q_rsem.at[i], to)
        copy.start()
        sent.append(copy)

    def q_wait(i):
        remote(q_block(i), q_block(i), q_ssem.at[0], q_rsem.at[i], mate).wait_recv()

    for ra in range(1, A):
        q_send(me, index(a + ra, b, c))
    for rb in range(1, B):
        q_send(me, index(a, b + rb, c))
    q_send(me, mate)
    for d in range(n):
        w_copy(d).start()

    count = slots * GROUP
    lane = lax.broadcasted_iota(jnp.int32, (seqs, 128), 1)
    named = jnp.zeros((seqs, 128), F32)
    left = jnp.zeros((seqs, 128), F32)
    lengths = pages_ref[:, max_pages : max_pages + 1]
    for j in range(max_pages):
        hit = jnp.logical_and(pages_ref[:, j : j + 1] - me * slots == lane, lane < slots)
        named = jnp.where(hit, 1.0, named)
        seen = jnp.clip(lengths - j * page_len, 0, page_len).astype(F32)
        left = jnp.where(hit, seen, left)
    row_slot = jnp.where(
        lax.broadcasted_iota(jnp.int32, (count, 128), 0) // GROUP
        == lax.broadcasted_iota(jnp.int32, (count, 128), 1),
        1.0, 0.0,
    ).astype(BF16)

    def rows_of(x):
        return lax.dot_general(
            row_slot, x.astype(BF16), (((1,), (1,)), ((), ())), preferred_element_type=F32
        )

    wide = rows_of(jnp.concatenate([named] * GROUP, axis=0))
    own_lane = lax.broadcasted_iota(jnp.int32, (count, GROUP * seqs), 1) // seqs
    own_row = lax.broadcasted_iota(jnp.int32, (count, GROUP * seqs), 0) % GROUP
    pick[...] = jnp.where(own_lane == own_row, wide, 0.0).astype(BF16)
    left = jnp.broadcast_to(jnp.sum(left, axis=0, keepdims=True), (page_len, 128))
    token = lax.broadcasted_iota(jnp.int32, (count, page_len), 1).astype(F32)
    mask[...] = jnp.where(token < rows_of(left), 1.0, 0.0)
    to_row = lax.broadcasted_iota(jnp.int32, (count, count), 0)
    from_row = lax.broadcasted_iota(jnp.int32, (count, count), 1)
    perm[...] = jnp.where(
        jnp.logical_and(to_row // slots == from_row % GROUP, to_row % slots == from_row // GROUP),
        1.0, 0.0,
    ).astype(BF16)

    for p in range(slots):
        kv_copy(p).wait()

    spread = jnp.where(
        lax.broadcasted_iota(jnp.int32, (slots, 1, 128), 2)
        == lax.rem(me * slots, 128) + lax.broadcasted_iota(jnp.int32, (slots, 1, 128), 0),
        1.0, 0.0,
    )
    block = own_heads * slots

    def acc_copy(o):
        return remote(
            acc_send.at[pl.ds(pl.multiple_of(o * block, 16), block), :], acc_recv.at[me],
            acc_ssem.at[o], acc_rsem.at[me], o,
        )

    def ml_copy(o):
        return remote(ml_send.at[o], ml_recv.at[me], ml_ssem.at[o], ml_rsem.at[me], o)

    ml_send[...] = jnp.zeros_like(ml_send)

    def attend(k):
        at = pl.multiple_of(k * HEAD_DIM, HEAD_DIM)
        mine = qall[pl.ds(pl.multiple_of(k * GROUP * seqs, GROUP * seqs), GROUP * seqs), :]
        query = jnp.dot(pick[...], mine, preferred_element_type=F32).astype(BF16)
        query = query.reshape(slots, GROUP, HEAD_DIM)
        keys = kv[:, :, pl.ds(at, HEAD_DIM)]
        values = kv[:, :, pl.ds(pl.multiple_of(KV_HEADS * HEAD_DIM + at, 128), HEAD_DIM)]
        score = jnp.einsum("phd,ptd->pht", query, keys, preferred_element_type=F32)
        seen = mask[...].reshape(slots, GROUP, page_len)
        score = jnp.where(seen > 0, score * HEAD_DIM**-0.5, NEG)
        top = jnp.max(score, axis=2, keepdims=True)
        weight = jnp.exp(score - top) * seen
        share = jnp.sum(weight, axis=2, keepdims=True)
        acc = jnp.einsum("pht,ptd->phd", weight.astype(BF16), values, preferred_element_type=F32)
        share = jnp.maximum(share, 1e-30)
        acc = acc * (1.0 / share)
        top = top + jnp.log(share)
        acc = jnp.dot(
            perm[...], acc.reshape(count, HEAD_DIM).astype(BF16), preferred_element_type=F32
        )
        acc_send[pl.ds(pl.multiple_of(k * count, count), count), :] = acc.astype(BF16)
        top = jnp.sum(top * spread, axis=0)
        for j in range(owners):
            o = k * owners + j
            ml_send[o, 0:own_heads, :] = top[j * own_heads : (j + 1) * own_heads]

            @pl.when(o != me)
            def _():
                acc_copy(o).start()
                ml_copy(o).start()

    near = [ra for ra in (1, A - 1) if 0 < ra < A]
    turns = list(dict.fromkeys(near + list(range(1, A))))
    chips = n // 2

    def ready(ra, rb):
        q_wait(index(a + ra, b + rb, 1 - c))
        if chips == KV_HEADS:
            attend(index(a + ra, b + rb, 0) // 2)

    ready(0, 0)
    for rb in range(1, B):
        i = index(a, b + rb, c)
        q_wait(i)
        q_send(i, mate)
    for rb in range(1, B):
        ready(0, rb)
    for ra in turns:
        i = index(a + ra, b, c)
        q_wait(i)
        for rb in range(1, B):
            q_send(i, index(a, b + rb, c))
        q_send(i, mate)
    for ra in turns:
        ready(ra, 0)
    for ra in turns:
        for rb in range(1, B):
            i = index(a + ra, b + rb, c)
            q_wait(i)
            q_send(i, mate)
    for ra in turns:
        for rb in range(1, B):
            ready(ra, rb)
    if chips != KV_HEADS:

        def one_head(k, carry):
            attend(k)
            return carry

        lax.fori_loop(0, KV_HEADS, one_head, 0)
    acc_recv[me] = acc_send[pl.ds(pl.multiple_of(me * block, 16), block), :]
    ml_recv[me] = ml_send[me]

    for step in range(1, n):
        i = lax.rem(me + step, n)
        remote(acc_recv.at[i], acc_recv.at[i], acc_ssem.at[i], acc_rsem.at[i], i).wait_recv()
        remote(ml_recv.at[i], ml_recv.at[i], ml_ssem.at[i], ml_rsem.at[i], i).wait_recv()

    all_slots = n * slots
    slot_id = lax.broadcasted_iota(jnp.int32, (seqs, all_slots), 1)
    named = jnp.zeros((seqs, all_slots), F32)
    for j in range(max_pages):
        named = jnp.where(pages_ref[:, j : j + 1] == slot_id, 1.0, named)
    per = 128 // slots
    ml_all = jnp.concatenate(
        [jnp.sum(ml_recv[g * per : (g + 1) * per], axis=0) for g in range(n // per)], axis=1
    )
    for h in range(own_heads):
        top_row = ml_all[h : h + 1, :]
        top = jnp.max(jnp.where(named > 0, top_row, -3e38), axis=1, keepdims=True)
        scale = jnp.where(named > 0, jnp.exp(jnp.minimum(top_row - top, 0.0)), 0.0).astype(BF16)
        whole = jnp.sum(scale.astype(F32), axis=1, keepdims=True)
        acc = acc_recv[:, h * slots : (h + 1) * slots, :].reshape(all_slots, HEAD_DIM)
        acc = jnp.dot(scale, acc, preferred_element_type=F32)
        att[:, h * HEAD_DIM : (h + 1) * HEAD_DIM] = (acc / whole).astype(BF16)


    def project(d):
        w_copy(d).wait()
        at = pl.ds(pl.multiple_of(d * cols, 128), cols)
        return jnp.dot(att[...], w[:, at], preferred_element_type=F32)

    def part1(t):
        return remote(part1_send.at[t], part1_recv.at[t], s1_ssem.at[t], s1_rsem.at[t], mate)

    def part2(ra, rb):
        t = ra * (B - 1) + rb - 1
        return remote(
            part2_send.at[t], part2_recv.at[t], s2_ssem.at[t], s2_rsem.at[t],
            index(a, b + rb, c),
        )

    def part3(ra):
        t = ra - 1
        return remote(
            part3_send.at[t], part3_recv.at[t], s3_ssem.at[t], s3_rsem.at[t],
            index(a + ra, b, c),
        )

    def give(ra, rb):
        t = ra * B + rb
        part1_send[t] = project(index(a + ra, b + rb, 1 - c)).astype(BF16)
        part1(t).start()

    def keep(ra, rb):
        value = project(index(a + ra, b + rb, c))
        part1(ra * B + rb).wait_recv()
        return value + part1_recv[ra * B + rb].astype(F32)

    def finish(ra):
        value = keep(ra, 0)
        for other in range(1, B):
            part2(ra, other).wait_recv()
            value = value + part2_recv[ra * (B - 1) + other - 1].astype(F32)
        if ra:
            part3_send[ra - 1] = value.astype(BF16)
            part3(ra).start()
            return
        for other in range(1, A):
            part3(other).wait_recv()
            value = value + part3_recv[other - 1].astype(F32)
        out_ref[...] = value.astype(BF16)

    turns = list(range(1, A)) + [0]
    before = None
    for ra in turns:
        for rb in list(range(1, B)) + [0]:
            give(ra, rb)
        for rb in range(1, B):
            part2_send[ra * (B - 1) + rb - 1] = keep(ra, rb).astype(BF16)
            part2(ra, rb).start()
        if before is not None:
            finish(before)
        before = ra
    finish(0)
    order = [(ra, rb) for ra in range(A) for rb in range(B)]

    for copy in sent:
        copy.wait_send()
    for step in range(1, n):
        o = lax.rem(me + step, n)
        acc_copy(o).wait_send()
        ml_copy(o).wait_send()
    for ra, rb in order:
        part1(ra * B + rb).wait_send()
        if rb:
            part2(ra, rb).wait_send()
        elif ra:
            part3(ra).wait_send()


def shards(n, queries, kv_pages, page_table, lengths, out_weight):
    slots, page_len, width = kv_pages.shape
    seqs, max_pages = page_table.shape
    A, B = grid_of(n)
    own_heads = HEADS // n
    padded = max(own_heads, 8)
    depth, features = out_weight.shape
    cols = features // n
    block = own_heads * slots
    pages = jnp.concatenate([page_table, lengths[:, None]], axis=1)
    vmem = pl.BlockSpec(memory_space=pltpu.VMEM)
    hbm = pl.BlockSpec(memory_space=pl.ANY)
    dma = pltpu.SemaphoreType.DMA
    q_sends = (A - 1) + (B - 1) + 1 + (A - 1) * B + A * (B - 1)
    return pl.pallas_call(
        functools.partial(kernel, n),
        out_shape=jax.ShapeDtypeStruct((seqs, cols), BF16),
        in_specs=[vmem, hbm, vmem, hbm],
        out_specs=vmem,
        scratch_shapes=[
            pltpu.VMEM((slots, page_len, width), BF16),
            pltpu.VMEM((depth, features), BF16),
            pltpu.VMEM((HEADS * seqs, HEAD_DIM), BF16),
            pltpu.VMEM((slots * GROUP, GROUP * seqs), BF16),
            pltpu.VMEM((slots * GROUP, page_len), F32),
            pltpu.VMEM((slots * GROUP, slots * GROUP), BF16),
            pltpu.VMEM((seqs, depth), BF16),
            pltpu.VMEM((HEADS * slots, HEAD_DIM), BF16),
            pltpu.VMEM((n, block, HEAD_DIM), BF16),
            pltpu.VMEM((n, padded, 128), F32),
            pltpu.VMEM((n, padded, 128), F32),
            pltpu.VMEM((A * B, seqs, cols), BF16),
            pltpu.VMEM((A * B, seqs, cols), BF16),
            pltpu.VMEM((A * (B - 1), seqs, cols), BF16),
            pltpu.VMEM((A * (B - 1), seqs, cols), BF16),
            pltpu.VMEM((A - 1, seqs, cols), BF16),
            pltpu.VMEM((A - 1, seqs, cols), BF16),
            dma((slots,)), dma((n,)), dma((q_sends,)), dma((n,)),
            dma((n,)), dma((n,)), dma((n,)), dma((n,)),
            dma((A * B,)), dma((A * B,)),
            dma((A * (B - 1),)), dma((A * (B - 1),)),
            dma((A - 1,)), dma((A - 1,)),
        ],
        compiler_params=pltpu.CompilerParams(
            collective_id=0, has_side_effects=True, vmem_limit_bytes=60 * 1024 * 1024
        ),
        name="paged_decode",
    )(queries, kv_pages, pages, out_weight)


def solution(mesh):
    placed = (
        P("parts", "pool"),
        P(("parts", "pool"), None, None),
        P("parts", None),
        P("parts"),
        P("pool", None),
    )
    return jax.shard_map(
        functools.partial(shards, mesh.shape["pool"]), mesh=mesh, in_specs=placed,
        out_specs=P("parts", "pool"), check_vma=False,
    )
```

```python
import functools

import jax
import jax.numpy as jnp
from jax import lax
from jax.experimental import pallas as pl
from jax.experimental.pallas import tpu as pltpu
from jax.sharding import PartitionSpec as P

HEADS = 128
KV_HEADS = 8
HEAD_DIM = 128
GROUP = HEADS // KV_HEADS
NEG = -1e30
F32 = jnp.float32
BF16 = jnp.bfloat16


def grid_of(n):
    chips = n // 2
    outer = 1
    while outer * outer < chips:
        outer *= 2
    return outer, chips // outer


def kernel(
    n, q_ref, kv_hbm, pages_ref, w_hbm, out_ref,
    kv, w, qall, pick, mask, perm, att,
    acc_send, acc_recv, ml_send, ml_recv,
    part1_send, part1_recv, part2_send, part2_recv, part3_send, part3_recv,
    kv_sem, w_sem, q_ssem, q_rsem, acc_ssem, acc_rsem, ml_ssem, ml_rsem,
    s1_ssem, s1_rsem, s2_ssem, s2_rsem, s3_ssem, s3_rsem,
):
    A, B = grid_of(n)
    me = lax.axis_index("pool")
    c = lax.rem(me, 2)
    b = lax.rem(me // 2, B)
    a = me // (2 * B)
    slots, page_len = kv.shape[0], kv.shape[1]
    seqs = q_ref.shape[0]
    max_pages = pages_ref.shape[1] - 1
    own_heads = HEADS // n
    padded = max(own_heads, 8)
    owners = n // KV_HEADS
    rows = own_heads * seqs
    cols = w.shape[1] // n

    def index(x, y, z):
        return (lax.rem(x, A) * B + lax.rem(y, B)) * 2 + z

    def remote(src, dst, ssem, rsem, to):
        return pltpu.make_async_remote_copy(
            src_ref=src, dst_ref=dst, send_sem=ssem, recv_sem=rsem,
            device_id={"pool": to}, device_id_type=pl.DeviceIdType.MESH,
        )

    def kv_copy(p):
        return pltpu.make_async_copy(kv_hbm.at[p], kv.at[p], kv_sem.at[p])

    def w_copy(d):
        span = pl.ds(pl.multiple_of(d * cols, 128), cols)
        return pltpu.make_async_copy(w_hbm.at[:, span], w.at[:, span], w_sem.at[d])

    barrier = pltpu.get_barrier_semaphore()
    for step in range(1, n):
        pl.semaphore_signal(
            barrier, inc=1, device_id={"pool": lax.rem(me + step, n)},
            device_id_type=pl.DeviceIdType.MESH,
        )
    for p in range(slots):
        kv_copy(p).start()

    half = rows // 2

    def q_block(i, f):
        return qall.at[pl.ds(pl.multiple_of(i * rows + f * half, 16), half), :]

    for h in range(own_heads):
        qall[pl.ds(pl.multiple_of(me * rows + h * seqs, 32), seqs), :] = q_ref[
            :, h * HEAD_DIM : (h + 1) * HEAD_DIM
        ]
    pl.semaphore_wait(barrier, n - 1)

    mate = index(a, b, 1 - c)
    sent = []

    def q_send(i, f, to):
        copy = remote(
            q_block(i, f), q_block(i, f), q_ssem.at[len(sent)], q_rsem.at[2 * i + f], to
        )
        copy.start()
        sent.append(copy)

    def q_wait(i, f):
        remote(q_block(i, f), q_block(i, f), q_ssem.at[0], q_rsem.at[2 * i + f], mate).wait_recv()

    for f in range(2):
        for ra in range(1, A):
            q_send(me, f, index(a + ra, b, c))
        for rb in range(1, B):
            q_send(me, f, index(a, b + rb, c))
        q_send(me, f, mate)
    for d in range(n):
        w_copy(d).start()

    count = slots * GROUP
    lane = lax.broadcasted_iota(jnp.int32, (seqs, 128), 1)
    named = jnp.zeros((seqs, 128), F32)
    left = jnp.zeros((seqs, 128), F32)
    lengths = pages_ref[:, max_pages : max_pages + 1]
    for j in range(max_pages):
        hit = jnp.logical_and(pages_ref[:, j : j + 1] - me * slots == lane, lane < slots)
        named = jnp.where(hit, 1.0, named)
        seen = jnp.clip(lengths - j * page_len, 0, page_len).astype(F32)
        left = jnp.where(hit, seen, left)
    row_slot = jnp.where(
        lax.broadcasted_iota(jnp.int32, (count, 128), 0) // GROUP
        == lax.broadcasted_iota(jnp.int32, (count, 128), 1),
        1.0, 0.0,
    ).astype(BF16)

    def rows_of(x):
        return lax.dot_general(
            row_slot, x.astype(BF16), (((1,), (1,)), ((), ())), preferred_element_type=F32
        )

    wide = rows_of(jnp.concatenate([named] * GROUP, axis=0))
    own_lane = lax.broadcasted_iota(jnp.int32, (count, GROUP * seqs), 1) // seqs
    own_row = lax.broadcasted_iota(jnp.int32, (count, GROUP * seqs), 0) % GROUP
    pick[...] = jnp.where(own_lane == own_row, wide, 0.0).astype(BF16)
    left = jnp.broadcast_to(jnp.sum(left, axis=0, keepdims=True), (page_len, 128))
    token = lax.broadcasted_iota(jnp.int32, (count, page_len), 1).astype(F32)
    mask[...] = jnp.where(token < rows_of(left), 1.0, 0.0)
    to_row = lax.broadcasted_iota(jnp.int32, (count, count), 0)
    from_row = lax.broadcasted_iota(jnp.int32, (count, count), 1)
    perm[...] = jnp.where(
        jnp.logical_and(to_row // slots == from_row % GROUP, to_row % slots == from_row // GROUP),
        1.0, 0.0,
    ).astype(BF16)

    for p in range(slots):
        kv_copy(p).wait()

    spread = jnp.where(
        lax.broadcasted_iota(jnp.int32, (slots, 1, 128), 2)
        == lax.rem(me * slots, 128) + lax.broadcasted_iota(jnp.int32, (slots, 1, 128), 0),
        1.0, 0.0,
    )
    block = own_heads * slots

    def acc_copy(o):
        return remote(
            acc_send.at[pl.ds(pl.multiple_of(o * block, 16), block), :], acc_recv.at[me],
            acc_ssem.at[o], acc_rsem.at[me], o,
        )

    def ml_copy(o):
        return remote(ml_send.at[o], ml_recv.at[me], ml_ssem.at[o], ml_rsem.at[me], o)

    ml_send[...] = jnp.zeros_like(ml_send)

    def attend(k):
        at = pl.multiple_of(k * HEAD_DIM, HEAD_DIM)
        mine = qall[pl.ds(pl.multiple_of(k * GROUP * seqs, GROUP * seqs), GROUP * seqs), :]
        query = jnp.dot(pick[...], mine, preferred_element_type=F32).astype(BF16)
        query = query.reshape(slots, GROUP, HEAD_DIM)
        keys = kv[:, :, pl.ds(at, HEAD_DIM)]
        values = kv[:, :, pl.ds(pl.multiple_of(KV_HEADS * HEAD_DIM + at, 128), HEAD_DIM)]
        score = jnp.einsum("phd,ptd->pht", query, keys, preferred_element_type=F32)
        seen = mask[...].reshape(slots, GROUP, page_len)
        score = jnp.where(seen > 0, score * HEAD_DIM**-0.5, NEG)
        top = jnp.max(score, axis=2, keepdims=True)
        weight = jnp.exp(score - top) * seen
        share = jnp.sum(weight, axis=2, keepdims=True)
        acc = jnp.einsum("pht,ptd->phd", weight.astype(BF16), values, preferred_element_type=F32)
        share = jnp.maximum(share, 1e-30)
        acc = acc * (1.0 / share)
        top = top + jnp.log(share)
        acc = jnp.dot(
            perm[...], acc.reshape(count, HEAD_DIM).astype(BF16), preferred_element_type=F32
        )
        acc_send[pl.ds(pl.multiple_of(k * count, count), count), :] = acc.astype(BF16)
        top = jnp.sum(top * spread, axis=0)
        for j in range(owners):
            o = k * owners + j
            ml_send[o, 0:own_heads, :] = top[j * own_heads : (j + 1) * own_heads]

            @pl.when(o != me)
            def _():
                acc_copy(o).start()
                ml_copy(o).start()

    near = [ra for ra in (1, A - 1) if 0 < ra < A]
    turns = list(dict.fromkeys(near + list(range(1, A))))
    chips = n // 2

    def ready(ra, rb):
        for f in range(2):
            q_wait(index(a + ra, b + rb, 1 - c), f)
        if chips == KV_HEADS:
            attend(index(a + ra, b + rb, 0) // 2)

    ready(0, 0)
    for rb in range(1, B):
        i = index(a, b + rb, c)
        for f in range(2):
            q_wait(i, f)
            q_send(i, f, mate)
    for rb in range(1, B):
        ready(0, rb)
    for f in range(2):
        for ra in turns:
            i = index(a + ra, b, c)
            q_wait(i, f)
            for rb in range(1, B):
                q_send(i, f, index(a, b + rb, c))
            q_send(i, f, mate)
    for ra in turns:
        ready(ra, 0)
    for ra in turns:
        for rb in range(1, B):
            i = index(a + ra, b + rb, c)
            for f in range(2):
                q_wait(i, f)
                q_send(i, f, mate)
    for ra in turns:
        for rb in range(1, B):
            ready(ra, rb)
    if chips != KV_HEADS:

        def one_head(k, carry):
            attend(k)
            return carry

        lax.fori_loop(0, KV_HEADS, one_head, 0)
    acc_recv[me] = acc_send[pl.ds(pl.multiple_of(me * block, 16), block), :]
    ml_recv[me] = ml_send[me]

    for step in range(1, n):
        i = lax.rem(me + step, n)
        remote(acc_recv.at[i], acc_recv.at[i], acc_ssem.at[i], acc_rsem.at[i], i).wait_recv()
        remote(ml_recv.at[i], ml_recv.at[i], ml_ssem.at[i], ml_rsem.at[i], i).wait_recv()

    all_slots = n * slots
    slot_id = lax.broadcasted_iota(jnp.int32, (seqs, all_slots), 1)
    named = jnp.zeros((seqs, all_slots), F32)
    for j in range(max_pages):
        named = jnp.where(pages_ref[:, j : j + 1] == slot_id, 1.0, named)
    per = 128 // slots
    ml_all = jnp.concatenate(
        [jnp.sum(ml_recv[g * per : (g + 1) * per], axis=0) for g in range(n // per)], axis=1
    )
    for h in range(own_heads):
        top_row = ml_all[h : h + 1, :]
        top = jnp.max(jnp.where(named > 0, top_row, -3e38), axis=1, keepdims=True)
        scale = jnp.where(named > 0, jnp.exp(jnp.minimum(top_row - top, 0.0)), 0.0).astype(BF16)
        whole = jnp.sum(scale.astype(F32), axis=1, keepdims=True)
        acc = acc_recv[:, h * slots : (h + 1) * slots, :].reshape(all_slots, HEAD_DIM)
        acc = jnp.dot(scale, acc, preferred_element_type=F32)
        att[:, h * HEAD_DIM : (h + 1) * HEAD_DIM] = (acc / whole).astype(BF16)


    def project(d):
        w_copy(d).wait()
        at = pl.ds(pl.multiple_of(d * cols, 128), cols)
        return jnp.dot(att[...], w[:, at], preferred_element_type=F32)

    def part1(t):
        return remote(part1_send.at[t], part1_recv.at[t], s1_ssem.at[t], s1_rsem.at[t], mate)

    def part2(ra, rb):
        t = ra * (B - 1) + rb - 1
        return remote(
            part2_send.at[t], part2_recv.at[t], s2_ssem.at[t], s2_rsem.at[t],
            index(a, b + rb, c),
        )

    def part3(ra):
        t = ra - 1
        return remote(
            part3_send.at[t], part3_recv.at[t], s3_ssem.at[t], s3_rsem.at[t],
            index(a + ra, b, c),
        )

    def give(ra, rb):
        t = ra * B + rb
        part1_send[t] = project(index(a + ra, b + rb, 1 - c)).astype(BF16)
        part1(t).start()

    def keep(ra, rb):
        value = project(index(a + ra, b + rb, c))
        part1(ra * B + rb).wait_recv()
        return value + part1_recv[ra * B + rb].astype(F32)

    def finish(ra):
        value = keep(ra, 0)
        for other in range(1, B):
            part2(ra, other).wait_recv()
            value = value + part2_recv[ra * (B - 1) + other - 1].astype(F32)
        if ra:
            part3_send[ra - 1] = value.astype(BF16)
            part3(ra).start()
            return
        for other in range(1, A):
            part3(other).wait_recv()
            value = value + part3_recv[other - 1].astype(F32)
        out_ref[...] = value.astype(BF16)

    turns = list(range(1, A)) + [0]
    before = None
    for ra in turns:
        for rb in list(range(1, B)) + [0]:
            give(ra, rb)
        for rb in range(1, B):
            part2_send[ra * (B - 1) + rb - 1] = keep(ra, rb).astype(BF16)
            part2(ra, rb).start()
        if before is not None:
            finish(before)
        before = ra
    finish(0)
    order = [(ra, rb) for ra in range(A) for rb in range(B)]

    for copy in sent:
        copy.wait_send()
    for step in range(1, n):
        o = lax.rem(me + step, n)
        acc_copy(o).wait_send()
        ml_copy(o).wait_send()
    for ra, rb in order:
        part1(ra * B + rb).wait_send()
        if rb:
            part2(ra, rb).wait_send()
        elif ra:
            part3(ra).wait_send()


def shards(n, queries, kv_pages, page_table, lengths, out_weight):
    slots, page_len, width = kv_pages.shape
    seqs, max_pages = page_table.shape
    A, B = grid_of(n)
    own_heads = HEADS // n
    padded = max(own_heads, 8)
    depth, features = out_weight.shape
    cols = features // n
    block = own_heads * slots
    pages = jnp.concatenate([page_table, lengths[:, None]], axis=1)
    vmem = pl.BlockSpec(memory_space=pltpu.VMEM)
    hbm = pl.BlockSpec(memory_space=pl.ANY)
    dma = pltpu.SemaphoreType.DMA
    q_sends = 2 * ((A - 1) + (B - 1) + 1 + (A - 1) * B + A * (B - 1))
    return pl.pallas_call(
        functools.partial(kernel, n),
        out_shape=jax.ShapeDtypeStruct((seqs, cols), BF16),
        in_specs=[vmem, hbm, vmem, hbm],
        out_specs=vmem,
        scratch_shapes=[
            pltpu.VMEM((slots, page_len, width), BF16),
            pltpu.VMEM((depth, features), BF16),
            pltpu.VMEM((HEADS * seqs, HEAD_DIM), BF16),
            pltpu.VMEM((slots * GROUP, GROUP * seqs), BF16),
            pltpu.VMEM((slots * GROUP, page_len), F32),
            pltpu.VMEM((slots * GROUP, slots * GROUP), BF16),
            pltpu.VMEM((seqs, depth), BF16),
            pltpu.VMEM((HEADS * slots, HEAD_DIM), BF16),
            pltpu.VMEM((n, block, HEAD_DIM), BF16),
            pltpu.VMEM((n, padded, 128), F32),
            pltpu.VMEM((n, padded, 128), F32),
            pltpu.VMEM((A * B, seqs, cols), BF16),
            pltpu.VMEM((A * B, seqs, cols), BF16),
            pltpu.VMEM((A * (B - 1), seqs, cols), BF16),
            pltpu.VMEM((A * (B - 1), seqs, cols), BF16),
            pltpu.VMEM((A - 1, seqs, cols), BF16),
            pltpu.VMEM((A - 1, seqs, cols), BF16),
            dma((slots,)), dma((n,)), dma((q_sends,)), dma((2 * n,)),
            dma((n,)), dma((n,)), dma((n,)), dma((n,)),
            dma((A * B,)), dma((A * B,)),
            dma((A * (B - 1),)), dma((A * (B - 1),)),
            dma((A - 1,)), dma((A - 1,)),
        ],
        compiler_params=pltpu.CompilerParams(
            collective_id=0, has_side_effects=True, vmem_limit_bytes=60 * 1024 * 1024
        ),
        name="paged_decode",
    )(queries, kv_pages, pages, out_weight)


def solution(mesh):
    placed = (
        P("parts", "pool"),
        P(("parts", "pool"), None, None),
        P("parts", None),
        P("parts"),
        P("pool", None),
    )
    return jax.shard_map(
        functools.partial(shards, mesh.shape["pool"]), mesh=mesh, in_specs=placed,
        out_specs=P("parts", "pool"), check_vma=False,
    )
```
